32 devices in a mesh: grp: 4 (over z), exp: 2 (over x), ten: 4 (over y, core).
Axes of the slice: x: 2, y: 2, z: 4, core: 2. Of those that a mesh axis runs over, the one named last changes fastest.
Arguments:
- tokens: bfloat16 [1024, 4096], P(('grp', 'exp', 'ten')), parts along dimension 0, may hold values from -100 to 100
- norm_gain: float32 [4096], replicated, may hold values from 0.1 to 1.9
- expert_ids: int32 [1024, 8], P(('grp', 'exp', 'ten')), parts along dimension 0, may hold values from 0 to 15, as said below
- gate_prob: float32 [1024, 8], P(('grp', 'exp', 'ten')), parts along dimension 0, may hold values from 0.05 to 1
- w_gate: bfloat16 [16, 4096, 1536], P('exp', None, 'ten'), may hold values from -0.09375 to 0.09375
- w_up: bfloat16 [16, 4096, 1536], P('exp', None, 'ten'), may hold values from -0.09375 to 0.09375
- w_down: bfloat16 [16, 1536, 4096], P('exp', 'ten'), may hold values from -0.15625 to 0.15625
Outputs:
- mixed: bfloat16 [1024, 4096], P(('grp', 'exp', 'ten')), parts along dimension 0
The draws below stay inside these ranges and needn't reach their ends.
There are 4 independent parts, one for each index of `grp`. The reference program is written for one: setup_inputs(seed, part) draws one part's arguments, and reference() takes and returns one part's arrays. A program takes and returns all parts, laid end to end along the dimension named above; an argument that names none is the same for every part. Nothing has to cross between parts.
Inputs may be any that keep to these rules, and one draw needn't show every extreme that they name: `expert_ids`: each row names 8 different experts. Within the rows of one device no expert is named by more than 24 rows, and in every draw one expert is named by exactly 24 rows of every device.
All inputs are finite; a program needn't handle non-finite values.
Results may differ from the reference program's by a relative error of at most 0.012.
Values may be sent and summed in bfloat16 or wider, within the bound.
No kernel may reach another device: no remote copies, remote signals or barrier semaphores. Data moves between devices by JAX's collectives and lax.ppermute only.
A program may use at most 192 MiB of HBM per device.

```python
import math
import jax
import jax.numpy as jnp
from jax import lax

D = 4096
FF = 1536
TOP = 8
EXPERTS = 16
TOK_DEV = 32
CAP = 24
TOKENS = 256
N_TEN = 4


def draw_tokens(key, part):
    key_rows, key_cols, key_base = jax.random.split(key, 3)
    row_scale = jnp.exp(jax.random.uniform(key_rows, (TOKENS, 1)) * math.log(10.0))
    col_scale = jnp.exp(jax.random.uniform(key_cols, (1, D)) * math.log(10.0))
    base_values = jnp.clip(jax.random.normal(key_base, (TOKENS, D)), -4.0, 4.0)
    return (base_values * row_scale * col_scale * 0.25).astype(jnp.bfloat16)


def shuffle_experts(block_key):
    return jax.random.permutation(block_key, EXPERTS)


def shuffle_tokens(block_key):
    return jax.random.permutation(block_key, TOK_DEV)


def pick_experts(order, columns):
    return order[columns]


def draw_expert_ids(key, part):
    blocks = TOKENS // TOK_DEV
    key_hot, key_perm, key_rank, key_start = jax.random.split(jax.random.fold_in(key, 7), 4)
    hot_expert = jax.random.randint(key_hot, (), 0, EXPERTS)
    orders = jax.vmap(shuffle_experts)(jax.random.split(key_perm, blocks))
    places = jnp.arange(EXPERTS, dtype=jnp.int32)[None, :]
    displaced = orders[:, TOP - 1:TOP]
    orders = jnp.where(orders == hot_expert, displaced, jnp.where(places == TOP - 1, hot_expert, orders))
    ranking = jax.vmap(shuffle_tokens)(jax.random.split(key_rank, blocks))
    free_start = jax.random.randint(key_start, (blocks, TOK_DEV), 0, TOP)
    window_start = jnp.where(ranking < TOK_DEV // 4, EXPERTS - 1, jnp.where(ranking < TOK_DEV // 2, TOP - 1, free_start))
    columns = (window_start[:, :, None] + jnp.arange(TOP, dtype=jnp.int32)[None, None, :]) % EXPERTS
    chosen = jax.vmap(pick_experts)(orders, columns)
    return chosen.reshape(TOKENS, TOP).astype(jnp.int32)


def block_levels(rng, dims, pieces, smallest, high):
    def one(axis_at, parts):
        heights = jax.random.uniform(jax.random.fold_in(jax.random.fold_in(rng, 6), axis_at), (parts,), jnp.float32, smallest / len(pieces), high / len(pieces))
        return jnp.repeat(jnp.exp(heights), dims[axis_at] // parts).reshape((-1,) + (1,) * (len(dims) - axis_at - 1))

    gain = one(*pieces[0])
    for cut in pieces[1:]:
        gain = gain * one(*cut)
    return gain


def scatter_about(key, dims, spread, most, pieces=(), kind=jnp.bfloat16):
    entries = jax.random.normal(key, dims, jnp.float32) * spread
    if len(pieces) > 0:
        entries = block_levels(key, dims, pieces, -0.22, 0.18) * entries
    return jnp.clip(entries, min=-most, max=most).astype(kind)


def setup_inputs(seed: int = 0, part: int = 0) -> dict:
    key_list = jax.random.split(jax.random.key(seed), 8)
    part_keys = jax.random.split(jax.random.fold_in(key_list[7], part), 8)
    tokens = draw_tokens(jax.random.fold_in(jax.random.fold_in(key_list[7], part), 71), part)
    norm_gain = jnp.clip(1.0 + 0.18 * jax.random.normal(key_list[1], (D,), jnp.float32), 0.1, 1.9)
    expert_ids = draw_expert_ids(jax.random.fold_in(jax.random.fold_in(key_list[7], part), 71), part)
    gate_prob = jnp.clip(jnp.exp(math.log(1.0) - 2.9957323 * jax.random.uniform(part_keys[3], (TOKENS, TOP), jnp.float32) ** block_levels(part_keys[3], (TOKENS, TOP), ((0, 8),), -0.2, 0.2)), 0.05, 1.0)
    w_gate = scatter_about(key_list[4], (EXPERTS, D, FF), D ** -0.5, 0.09375, ((0, 2), (2, 4)))
    w_up = scatter_about(key_list[5], (EXPERTS, D, FF), D ** -0.5, 0.09375, ((0, 2), (2, 4)))
    w_down = scatter_about(key_list[6], (EXPERTS, FF, D), FF ** -0.5, 0.15625, ((0, 2), (1, 4)))
    return {"tokens": tokens, "norm_gain": norm_gain, "expert_ids": expert_ids, "gate_prob": gate_prob, "w_gate": w_gate, "w_up": w_up, "w_down": w_down}


def expert_rows(rows, weight_gate, weight_up, weight_down):
    gate_part = jnp.dot(rows, weight_gate, preferred_element_type=jnp.float32)
    up_part = jnp.dot(rows, weight_up, preferred_element_type=jnp.float32)
    hidden = (jax.nn.silu(gate_part) * up_part).astype(jnp.bfloat16)
    group_width = FF // N_TEN
    total = jnp.zeros((rows.shape[0], D), jnp.float32)
    for group in range(N_TEN):
        lower = group * group_width
        upper = lower + group_width
        term = jnp.dot(hidden[:, lower:upper], weight_down[lower:upper], preferred_element_type=jnp.float32).astype(jnp.bfloat16)
        total = total + lax.optimization_barrier(term).astype(jnp.float32)
    return total.astype(jnp.bfloat16)

def reference(tokens, norm_gain, expert_ids, gate_prob, w_gate, w_up, w_down):
    floats = tokens.astype(jnp.float32)
    meansq = lax.optimization_barrier(jnp.mean(floats * floats, axis=1, keepdims=True))
    normed = (floats * lax.rsqrt(meansq + 1e-06) * norm_gain).astype(jnp.bfloat16)
    mixing = gate_prob / lax.optimization_barrier(jnp.sum(gate_prob, axis=1, keepdims=True))
    blocks = TOKENS // TOK_DEV
    assigned = TOK_DEV * TOP
    block_ids = expert_ids.reshape(blocks, assigned)
    member = (block_ids[:, :, None] == jnp.arange(EXPERTS, dtype=jnp.int32)[None, None, :]).astype(jnp.int32)
    earlier = jnp.cumsum(member, axis=1) - member
    slot_index = lax.optimization_barrier(jnp.sum(earlier * member, axis=2))
    target = (block_ids * CAP + slot_index).astype(jnp.int32)
    source_rows = normed.reshape(blocks, TOK_DEV, D)
    token_of = (jnp.arange(assigned, dtype=jnp.int32) // TOP).astype(jnp.int32)
    block_of = jnp.arange(blocks, dtype=jnp.int32)[:, None]
    buffer = jnp.zeros((blocks, EXPERTS * CAP, D), jnp.bfloat16)
    buffer = buffer.at[block_of, target].set(source_rows[:, token_of])
    per_expert = buffer.reshape(blocks, EXPERTS, CAP, D).transpose(1, 0, 2, 3).reshape(EXPERTS, blocks * CAP, D)
    outputs = lax.map(lambda item: expert_rows(item[0], item[1], item[2], item[3]), (per_expert, w_gate, w_up, w_down))
    outputs = outputs.reshape(EXPERTS, blocks, CAP, D).transpose(1, 0, 2, 3).reshape(blocks, EXPERTS * CAP, D)
    picked = outputs[block_of, target].reshape(TOKENS, TOP, D)
    mixed = lax.optimization_barrier(jnp.sum(mixing[:, :, None] * picked.astype(jnp.float32), axis=1))
    return mixed.astype(jnp.bfloat16)
```

```python
import jax
import jax.numpy as jnp
from jax import lax
from jax.sharding import PartitionSpec as P


def per_device(tokens, norm_gain, expert_ids, gate_prob, w_gate, w_up, w_down):
    tok_rows, width = tokens.shape
    local_count = w_gate.shape[0]
    floats = tokens.astype(jnp.float32)
    meansq = jnp.mean(floats * floats, axis=1, keepdims=True)
    normed = (floats * lax.rsqrt(meansq + 1e-06) * norm_gain).astype(jnp.bfloat16)
    mixing = gate_prob / jnp.sum(gate_prob, axis=1, keepdims=True)
    expert_count = local_count * lax.axis_size("exp")
    chosen = expert_ids[:, :, None] == jnp.arange(expert_count, dtype=jnp.int32)
    weight = jnp.sum(jnp.where(chosen, mixing[:, :, None], 0.0), axis=1)
    rows = lax.all_gather(normed, ("exp", "ten"), axis=0, tiled=True)
    weight = lax.all_gather(weight, ("exp", "ten"), axis=0, tiled=True)
    weight = lax.dynamic_slice_in_dim(weight, lax.axis_index("exp") * local_count, local_count, axis=1)
    gate_part = jnp.einsum("td,edf->etf", rows, w_gate, preferred_element_type=jnp.float32)
    up_part = jnp.einsum("td,edf->etf", rows, w_up, preferred_element_type=jnp.float32)
    hidden = (jax.nn.silu(gate_part) * up_part * weight.T[:, :, None]).astype(jnp.bfloat16)
    part = jnp.einsum("etf,efd->td", hidden, w_down, preferred_element_type=jnp.float32)
    return lax.psum_scatter(
        part.astype(jnp.bfloat16), ("exp", "ten"), scatter_dimension=0, tiled=True
    )


def solution(mesh):
    placed = (
        P(("grp", "exp", "ten"), None),
        P(),
        P(("grp", "exp", "ten"), None),
        P(("grp", "exp", "ten"), None),
        P("exp", None, "ten"),
        P("exp", None, "ten"),
        P("exp", "ten", None),
    )
    return jax.shard_map(
        per_device,
        mesh=mesh,
        in_specs=placed,
        out_specs=P(("grp", "exp", "ten"), None),
        check_vma=False,
    )
```

```python
import functools

import jax
import jax.numpy as jnp
from jax import lax
from jax.experimental import pallas as pl
from jax.experimental.pallas import tpu as pltpu
from jax.sharding import PartitionSpec as P

BF16 = jnp.bfloat16
F32 = jnp.float32
MIB = 2**20
GROUP = ("exp", "ten")
EXTRA = 128
IN_CHUNKS = 4
OUT_CHUNKS = 4
VMEM_FULL = pl.BlockSpec(memory_space=pltpu.VMEM)


def in_vmem(value):
    return pltpu.with_memory_space_constraint(value, pltpu.VMEM)


def in_hbm(value):
    return pltpu.with_memory_space_constraint(value, pltpu.HBM)


def exchange(value, size, mask):
    return lax.ppermute(value, GROUP, [(i, i ^ mask) for i in range(size)])


def after(value, other):
    return lax.optimization_barrier((value, other))[0]


def norm_body(expert_count, tok_ref, gain_ref, ids_ref, prob_ref, *outs):
    floats = tok_ref[...].astype(F32)
    meansq = jnp.mean(floats * floats, axis=1, keepdims=True)
    normed = (floats * lax.rsqrt(meansq + 1e-06) * gain_ref[...]).astype(BF16)
    prob = prob_ref[...]
    mixing = prob / jnp.sum(prob, axis=1, keepdims=True)
    lane = lax.broadcasted_iota(jnp.int32, (prob.shape[0], EXTRA), 1)
    weight = jnp.zeros((prob.shape[0], EXTRA), F32)
    for k in range(prob.shape[1]):
        weight = weight + jnp.where(
            lane % expert_count == ids_ref[:, k : k + 1], mixing[:, k : k + 1], 0.0
        )
    high = weight.astype(BF16).astype(F32)
    middle = (weight - high).astype(BF16).astype(F32)
    low = weight - high - middle
    piece = lane // expert_count
    packed = jnp.where(piece == 0, high, jnp.where(piece == 1, middle, jnp.where(piece == 2, low, 0.0)))
    step = normed.shape[1] // len(outs)
    for j, out in enumerate(outs):
        out[:, :step] = normed[:, j * step : (j + 1) * step]
    outs[-1][:, step:] = packed.astype(BF16)


def norm_call(tokens, norm_gain, expert_ids, gate_prob, expert_count):
    rows, width = tokens.shape
    step = width // IN_CHUNKS
    shapes = [
        pltpu.VMEM((rows, step + (EXTRA if j == IN_CHUNKS - 1 else 0)), BF16)
        for j in range(IN_CHUNKS)
    ]
    return pl.pallas_call(
        functools.partial(norm_body, expert_count),
        out_shape=shapes,
        in_specs=[VMEM_FULL] * 4,
        out_specs=[VMEM_FULL] * IN_CHUNKS,
    )(tokens, norm_gain.reshape(1, width), expert_ids, gate_prob)


def gate_up_body(first, last, step, hidden, expert_count, parts, *refs):
    pieces, refs = refs[:parts], refs[parts:]
    gate_ref, up_ref = refs[:2]
    total_ref = None if first else refs[2]
    out_ref, rows_ref = refs[-2:]
    expert = pl.program_id(0)

    @pl.when(expert == 0)
    def _():
        at = 0
        for piece in pieces:
            rows_ref[at : at + piece.shape[0]] = piece[...]
            at += piece.shape[0]

    weights = jnp.concatenate([gate_ref[0], up_ref[0]], axis=1)
    both = jnp.dot(rows_ref[:, :step], weights, preferred_element_type=F32)
    if not first:
        both = both + total_ref[expert]
    if not last:
        out_ref[expert] = both
        return
    gate, up = both[:, :hidden], both[:, hidden:]
    number = lax.axis_index("exp") * pl.num_programs(0) + expert
    row = lax.broadcasted_iota(jnp.int32, (EXTRA, hidden), 0)
    pick = jnp.where((row % expert_count == number) & (row < 3 * expert_count), 1.0, 0.0)
    mixing = jnp.dot(rows_ref[:, step:], pick.astype(BF16), preferred_element_type=F32)
    out_ref[...] = (gate / (1.0 + jnp.exp(-gate)) * up * mixing).astype(BF16)


def gate_up_call(j, pieces, w_gate, w_up, total, expert_count):
    first, last = j == 0, j == IN_CHUNKS - 1
    local, width, hidden = w_gate.shape
    step = width // IN_CHUNKS
    rows = sum(p.shape[0] for p in pieces)
    weight_spec = pl.BlockSpec((1, step, hidden), lambda e: (e, j, 0))
    totals = [] if first else [total]
    if last:
        out_shape = pltpu.VMEM((rows, local * hidden), BF16)
        out_spec = pl.BlockSpec((rows, hidden), lambda e: (0, e))
    else:
        out_shape = pltpu.VMEM((local, rows, 2 * hidden), F32)
        out_spec = VMEM_FULL
    return pl.pallas_call(
        functools.partial(gate_up_body, first, last, step, hidden, expert_count, len(pieces)),
        grid=(local,),
        out_shape=out_shape,
        in_specs=[VMEM_FULL] * len(pieces) + [weight_spec] * 2 + [VMEM_FULL] * len(totals),
        out_specs=out_spec,
        scratch_shapes=[pltpu.VMEM((rows, pieces[0].shape[1]), BF16)],
        input_output_aliases={} if first or last else {len(pieces) + 2: 0},
        compiler_params=pltpu.CompilerParams(vmem_limit_bytes=16 * MIB),
        cost_estimate=pl.CostEstimate(
            flops=4 * rows * step * hidden * local,
            bytes_accessed=4 * step * hidden * local,
            transcendentals=0,
        ),
    )(*[in_vmem(p) for p in pieces], in_hbm(w_gate), in_hbm(w_up), *[in_vmem(t) for t in totals])


def down_body(half, hidden_ref, weight_ref, keep_ref, send_ref):
    out = jnp.dot(hidden_ref[...], weight_ref[...], preferred_element_type=F32).astype(BF16)
    keep_ref[...] = out[:half]
    send_ref[...] = out[half:]


def down_call(j, hidden, w_down):
    rows, depth = hidden.shape
    width = w_down.shape[1]
    step = width // OUT_CHUNKS
    block = min(512, step)
    steps = step // block
    half = rows // 2
    return pl.pallas_call(
        functools.partial(down_body, half),
        grid=(steps,),
        out_shape=[pltpu.VMEM((half, step), BF16)] * 2,
        in_specs=[VMEM_FULL, pl.BlockSpec((depth, block), lambda n: (0, j * steps + n))],
        out_specs=[pl.BlockSpec((half, block), lambda n: (0, n))] * 2,
        compiler_params=pltpu.CompilerParams(vmem_limit_bytes=16 * MIB),
        cost_estimate=pl.CostEstimate(
            flops=2 * rows * depth * step, bytes_accessed=2 * depth * step, transcendentals=0
        ),
    )(in_vmem(hidden), in_hbm(w_down))


def pair_body(keep_ref, got_ref, *outs):
    rows = outs[0].shape[0]
    for k, out in enumerate(outs):
        at = slice(k * rows, (k + 1) * rows)
        out[...] = (keep_ref[at].astype(F32) + got_ref[at].astype(F32)).astype(BF16)


def pair_call(keep, got, rows):
    count = keep.shape[0] // rows
    return pl.pallas_call(
        pair_body,
        out_shape=[pltpu.VMEM((rows, keep.shape[1]), BF16)] * count,
        in_specs=[VMEM_FULL] * 2,
        out_specs=[VMEM_FULL] * count,
    )(in_vmem(keep), in_vmem(got))


def finish_body(*refs):
    ins, out_ref = refs[:-1], refs[-1]
    count = len(ins) // OUT_CHUNKS
    step = ins[0].shape[1]
    for j in range(OUT_CHUNKS):
        total = ins[j * count][...].astype(F32)
        for ref in ins[j * count + 1 : (j + 1) * count]:
            total = total + ref[...].astype(F32)
        out_ref[:, j * step : (j + 1) * step] = total.astype(BF16)


def finish_call(parts, rows, width):
    return pl.pallas_call(
        finish_body,
        out_shape=jax.ShapeDtypeStruct((rows, width), BF16),
        in_specs=[VMEM_FULL] * len(parts),
        out_specs=VMEM_FULL,
    )(*[in_vmem(p) for p in parts])


def per_device(tokens, norm_gain, expert_ids, gate_prob, w_gate, w_up, w_down):
    rows, width = tokens.shape
    local, _, hidden = w_gate.shape
    size = lax.axis_size("exp") * lax.axis_size("ten")
    expert_count = local * lax.axis_size("exp")
    far = range(2, size, 2)

    own = norm_call(tokens, norm_gain, expert_ids, gate_prob, expert_count)
    gathered = []
    for j in range(IN_CHUNKS):
        mine = own[j]
        if j >= 2:
            mine = after(mine, gathered[j - 2][-1])
        near = [mine] + [exchange(mine, size, mask) for mask in far]
        gathered.append(near + [exchange(jnp.concatenate(near, axis=0), size, 1)])
    total = None
    for j in range(IN_CHUNKS):
        total = gate_up_call(j, gathered[j], w_gate, w_up, total, expert_count)

    w_rows = w_down.reshape(local * hidden, width)
    parts = []
    for j in range(OUT_CHUNKS):
        keep, send = down_call(j, total, w_rows)
        blocks = pair_call(keep, exchange(send, size, 1), rows)
        parts += [blocks[0]] + [exchange(b, size, mask) for b, mask in zip(blocks[1:], far)]
    return finish_call(parts, rows, width)


def solution(mesh):
    placed = (
        P(("grp", "exp", "ten"), None),
        P(),
        P(("grp", "exp", "ten"), None),
        P(("grp", "exp", "ten"), None),
        P("exp", None, "ten"),
        P("exp", None, "ten"),
        P("exp", "ten", None),
    )
    return jax.shard_map(
        per_device,
        mesh=mesh,
        in_specs=placed,
        out_specs=P(("grp", "exp", "ten"), None),
        check_vma=False,
    )
```

```python
import functools

import jax
import jax.numpy as jnp
from jax import lax
from jax.experimental import pallas as pl
from jax.experimental.pallas import tpu as pltpu
from jax.sharding import PartitionSpec as P

BF16 = jnp.bfloat16
F32 = jnp.float32
MIB = 2**20
GROUP = ("exp", "ten")
EXTRA = 128
SLOTS = 4
OUT_CHUNKS = 2
VMEM_FULL = pl.BlockSpec(memory_space=pltpu.VMEM)
ANY_FULL = pl.BlockSpec(memory_space=pl.ANY)


def in_vmem(value):
    return pltpu.with_memory_space_constraint(value, pltpu.VMEM)


def in_hbm(value):
    return pltpu.with_memory_space_constraint(value, pltpu.HBM)


def params(rows, width):
    return pltpu.CompilerParams(vmem_limit_bytes=4 * MIB + 4 * rows * width)


def cost(flops, read):
    return pl.CostEstimate(flops=flops, bytes_accessed=read, transcendentals=0)


def exchange(value, size, mask):
    return lax.ppermute(value, GROUP, [(i, i ^ mask) for i in range(size)])


def after(value, other):
    return lax.optimization_barrier((value, other))[0]


def norm_body(expert_count, *refs):
    sources, out_ref, targets, sems = refs[:4], refs[4], refs[5:9], refs[9]
    copies = [
        pltpu.make_async_copy(source, target, sems.at[i])
        for i, (source, target) in enumerate(zip(sources, targets))
    ]
    for copy in copies:
        copy.start()
    for copy in copies:
        copy.wait()
    tok_ref, gain_ref, ids_ref, prob_ref = targets
    width = tok_ref.shape[1]
    floats = tok_ref[...].astype(F32)
    meansq = jnp.mean(floats * floats, axis=1, keepdims=True)
    out_ref[:, :width] = (floats * lax.rsqrt(meansq + 1e-06) * gain_ref[...]).astype(BF16)
    prob = prob_ref[...]
    mixing = prob / jnp.sum(prob, axis=0, keepdims=True)
    place = lax.broadcasted_iota(jnp.int32, (EXTRA, prob.shape[1]), 0)
    weight = jnp.zeros(place.shape, F32)
    for k in range(prob.shape[0]):
        weight = weight + jnp.where(
            place % expert_count == ids_ref[k : k + 1], mixing[k : k + 1], 0.0
        )
    high = weight.astype(BF16).astype(F32)
    middle = (weight - high).astype(BF16).astype(F32)
    low = weight - high - middle
    piece = place // expert_count
    packed = jnp.where(piece == 0, high, jnp.where(piece == 1, middle, jnp.where(piece == 2, low, 0.0)))
    out_ref[:, width:] = packed.T.astype(BF16)


def norm_call(tokens, norm_gain, expert_ids, gate_prob, expert_count, scoped):
    rows, width = tokens.shape
    args = (tokens, norm_gain.reshape(1, width), expert_ids.T, gate_prob.T)
    return pl.pallas_call(
        functools.partial(norm_body, expert_count),
        out_shape=pltpu.VMEM((rows, width + EXTRA), BF16),
        in_specs=[ANY_FULL] * 4,
        out_specs=VMEM_FULL,
        scratch_shapes=[pltpu.VMEM(v.shape, v.dtype) for v in args]
        + [pltpu.SemaphoreType.DMA((4,))],
        compiler_params=scoped,
    )(*[in_hbm(v) for v in args])


def fetch_body(slots, order_ref, gate_hbm, up_hbm, gate_out, up_out, done_ref, sems):
    del order_ref
    copies = []
    for e in range(slots):
        copies.append(pltpu.make_async_copy(gate_hbm.at[e], gate_out.at[e], sems.at[0, e]))
        copies.append(pltpu.make_async_copy(up_hbm.at[e], up_out.at[e], sems.at[1, e]))
    for copy in copies:
        copy.start()
    done_ref[...] = jnp.zeros_like(done_ref)
    for copy in copies:
        copy.wait()


def fetch_call(order, w_gate, w_up, scoped):
    local, width, hidden = w_gate.shape
    slots = min(SLOTS, local)
    return pl.pallas_call(
        functools.partial(fetch_body, slots),
        out_shape=[pltpu.VMEM((slots, width, hidden), BF16)] * 2 + [pltpu.VMEM((8, 128), F32)],
        in_specs=[ANY_FULL] * 3,
        out_specs=[VMEM_FULL] * 3,
        scratch_shapes=[pltpu.SemaphoreType.DMA((2, slots))],
        compiler_params=scoped,
        cost_estimate=cost(0, 8 * slots * width * hidden),
    )(order, in_hbm(w_gate), in_hbm(w_up))


def gate_up_body(expert_count, parts, *refs):
    pieces, refs = refs[:parts], refs[parts:]
    gate_hbm, up_hbm, down_hbm = refs[2:5]
    out_ref, down_ref, gate_ref, up_ref, rows_ref, sems, down_sems = refs[5:]
    slots, width, hidden = gate_ref.shape
    local = gate_hbm.shape[0]

    def copies(e):
        slot = e % slots
        return [
            pltpu.make_async_copy(gate_hbm.at[e], gate_ref.at[slot], sems.at[0, slot]),
            pltpu.make_async_copy(up_hbm.at[e], up_ref.at[slot], sems.at[1, slot]),
        ]

    def down_copy(e):
        at = slice(e * hidden, (e + 1) * hidden)
        return pltpu.make_async_copy(down_hbm.at[at], down_ref.at[at], down_sems.at[e])

    down_copy(0).start()
    down_copy(1).start()
    at = 0
    for piece in pieces:
        rows_ref[at : at + piece.shape[0]] = piece[...]
        at += piece.shape[0]

    row = lax.broadcasted_iota(jnp.int32, (EXTRA, hidden), 0)
    number = lax.axis_index("exp") * local

    def finish(e, both):
        gate, up = both[:, :hidden], both[:, hidden:]
        pick = jnp.where((row % expert_count == number + e) & (row < 3 * expert_count), 1.0, 0.0)
        mixing = jnp.dot(rows_ref[:, width:], pick.astype(BF16), preferred_element_type=F32)
        value = gate / (1.0 + jnp.exp(-gate)) * up * mixing
        out_ref[:, e * hidden : (e + 1) * hidden] = value.astype(BF16)

    for e in range(local):
        if e >= slots:
            for copy in copies(e):
                copy.wait()
        weights = jnp.concatenate([gate_ref[e % slots], up_ref[e % slots]], axis=1)
        both = jnp.dot(rows_ref[:, :width], weights, preferred_element_type=F32)
        if e + slots < local:
            for copy in copies(e + slots):
                copy.start()
        if e + 2 < local:
            down_copy(e + 2).start()
        finish(e, both)
    for e in range(local):
        down_copy(e).wait()


def gate_up_call(pieces, gate_slots, up_slots, w_gate, w_up, w_down, expert_count, scoped):
    slots, width, hidden = gate_slots.shape
    local = w_gate.shape[0]
    depth = w_down.shape[0]
    rows = sum(p.shape[0] for p in pieces)
    count = len(pieces)
    shape = pltpu.VMEM(gate_slots.shape, BF16)
    return pl.pallas_call(
        functools.partial(gate_up_body, expert_count, count),
        out_shape=[pltpu.VMEM((rows, depth), BF16), pltpu.VMEM((depth, width), BF16), shape, shape],
        in_specs=[VMEM_FULL] * (count + 2) + [ANY_FULL] * 3,
        out_specs=[VMEM_FULL] * 4,
        scratch_shapes=[
            pltpu.VMEM((rows, width + EXTRA), BF16),
            pltpu.SemaphoreType.DMA((2, slots)),
            pltpu.SemaphoreType.DMA((local,)),
        ],
        input_output_aliases={count: 2, count + 1: 3},
        compiler_params=scoped,
        cost_estimate=cost(4 * rows * width * hidden * local, 6 * width * hidden * local),
    )(
        *[in_vmem(v) for v in (*pieces, gate_slots, up_slots)],
        *[in_hbm(v) for v in (w_gate, w_up, w_down)],
    )[:2]


def down_body(half, start, hidden_ref, weight_ref, keep_ref, send_ref):
    block = 512
    for at in range(0, keep_ref.shape[1], block):
        to = slice(at, at + block)
        weights = weight_ref[:, start + at : start + at + block]
        out = jnp.dot(hidden_ref[...], weights, preferred_element_type=F32).astype(BF16)
        keep_ref[:, to] = out[:half]
        send_ref[:, to] = out[half:]


def down_call(hidden, weight, start, step, scoped):
    rows, depth = hidden.shape
    half = rows // 2
    return pl.pallas_call(
        functools.partial(down_body, half, start),
        out_shape=[pltpu.VMEM((half, step), BF16)] * 2,
        in_specs=[VMEM_FULL] * 2,
        out_specs=[VMEM_FULL] * 2,
        compiler_params=scoped,
        cost_estimate=cost(2 * rows * depth * step, 2 * depth * step),
    )(in_vmem(hidden), in_vmem(weight))


def pair_body(keep_ref, got_ref, *outs):
    rows = outs[0].shape[0]
    for k, out in enumerate(outs):
        at = slice(k * rows, (k + 1) * rows)
        out[...] = (keep_ref[at].astype(F32) + got_ref[at].astype(F32)).astype(BF16)


def pair_call(keep, got, rows, scoped):
    count = keep.shape[0] // rows
    return pl.pallas_call(
        pair_body,
        out_shape=[pltpu.VMEM((rows, keep.shape[1]), BF16)] * count,
        in_specs=[VMEM_FULL] * 2,
        out_specs=[VMEM_FULL] * count,
        compiler_params=scoped,
    )(in_vmem(keep), in_vmem(got))


def finish_body(chunks, *refs):
    ins, out_ref = refs[:-1], refs[-1]
    count = len(ins) // chunks
    step = ins[0].shape[1]
    for j in range(chunks):
        total = ins[j * count][...].astype(F32)
        for ref in ins[j * count + 1 : (j + 1) * count]:
            total = total + ref[...].astype(F32)
        out_ref[:, j * step : (j + 1) * step] = total.astype(BF16)


def finish_call(parts, chunks, rows, width, scoped):
    return pl.pallas_call(
        functools.partial(finish_body, chunks),
        out_shape=jax.ShapeDtypeStruct((rows, width), BF16),
        in_specs=[VMEM_FULL] * len(parts),
        out_specs=VMEM_FULL,
        compiler_params=scoped,
    )(*[in_vmem(p) for p in parts])


def per_device(tokens, norm_gain, expert_ids, gate_prob, w_gate, w_up, w_down):
    rows, width = tokens.shape
    local, _, hidden = w_gate.shape
    size = lax.axis_size("exp") * lax.axis_size("ten")
    expert_count = local * lax.axis_size("exp")
    far = range(2, size, 2)
    w_rows = w_down.reshape(local * hidden, width)

    scoped = params(size * rows, width)

    own = norm_call(tokens, norm_gain, expert_ids, gate_prob, expert_count, scoped)
    gate_slots, up_slots, fetched = fetch_call(own, w_gate, w_up, scoped)
    near = [own] + [after(exchange(own, size, mask), fetched) for mask in far]
    pieces = near + [exchange(piece, size, 1) for piece in near]
    mixed_hidden, weight = gate_up_call(
        pieces, gate_slots, up_slots, w_gate, w_up, w_rows, expert_count, scoped
    )
    step = width // OUT_CHUNKS
    parts = []
    for j in range(OUT_CHUNKS):
        keep, send = down_call(mixed_hidden, weight, j * step, step, scoped)
        blocks = pair_call(keep, exchange(send, size, 1), rows, scoped)
        parts += [blocks[0]] + [exchange(b, size, mask) for b, mask in zip(blocks[1:], far)]
    return finish_call(parts, OUT_CHUNKS, rows, width, scoped)


def solution(mesh):
    placed = (
        P(("grp", "exp", "ten"), None),
        P(),
        P(("grp", "exp", "ten"), None),
        P(("grp", "exp", "ten"), None),
        P("exp", None, "ten"),
        P("exp", None, "ten"),
        P("exp", "ten", None),
    )
    return jax.shard_map(
        per_device,
        mesh=mesh,
        in_specs=placed,
        out_specs=P(("grp", "exp", "ten"), None),
        check_vma=False,
    )
```

```python
import functools

import jax
import jax.numpy as jnp
from jax import lax
from jax.experimental import pallas as pl
from jax.experimental.pallas import tpu as pltpu
from jax.sharding import PartitionSpec as P

BF16 = jnp.bfloat16
F32 = jnp.float32
MIB = 2**20
GROUP = ("exp", "ten")
EXTRA = 128
SLOTS = 5
AHEAD = 5
VMEM_FULL = pl.BlockSpec(memory_space=pltpu.VMEM)
ANY_FULL = pl.BlockSpec(memory_space=pl.ANY)


def in_vmem(value):
    return pltpu.with_memory_space_constraint(value, pltpu.VMEM)


def in_hbm(value):
    return pltpu.with_memory_space_constraint(value, pltpu.HBM)


def params(rows, width):
    return pltpu.CompilerParams(vmem_limit_bytes=2 * MIB + 4 * rows * width)


def cost(flops, read):
    return pl.CostEstimate(flops=flops, bytes_accessed=read, transcendentals=0)


def exchange(value, size, mask):
    return lax.ppermute(value, GROUP, [(i, i ^ mask) for i in range(size)])


def after(value, other):
    return lax.optimization_barrier((value, other))[0]


def norm_body(expert_count, *refs):
    sources, out_ref, targets, sems = refs[:4], refs[4], refs[5:9], refs[9]
    copies = [
        pltpu.make_async_copy(source, target, sems.at[i])
        for i, (source, target) in enumerate(zip(sources, targets))
    ]
    for copy in copies:
        copy.start()
    for copy in copies:
        copy.wait()
    tok_ref, gain_ref, ids_ref, prob_ref = targets
    width = tok_ref.shape[1]
    floats = tok_ref[...].astype(F32)
    meansq = jnp.mean(floats * floats, axis=1, keepdims=True)
    out_ref[:, :width] = (floats * lax.rsqrt(meansq + 1e-06) * gain_ref[...]).astype(BF16)
    prob = prob_ref[...]
    mixing = prob / jnp.sum(prob, axis=0, keepdims=True)
    place = lax.broadcasted_iota(jnp.int32, (EXTRA, prob.shape[1]), 0)
    weight = jnp.zeros(place.shape, F32)
    for k in range(prob.shape[0]):
        weight = weight + jnp.where(
            place % expert_count == ids_ref[k : k + 1], mixing[k : k + 1], 0.0
        )
    high = weight.astype(BF16).astype(F32)
    middle = (weight - high).astype(BF16).astype(F32)
    low = weight - high - middle
    piece = place // expert_count
    packed = jnp.where(piece == 0, high, jnp.where(piece == 1, middle, jnp.where(piece == 2, low, 0.0)))
    out_ref[:, width:] = packed.T.astype(BF16)


def norm_call(tokens, norm_gain, expert_ids, gate_prob, expert_count, scoped):
    rows, width = tokens.shape
    args = (tokens, norm_gain.reshape(1, width), expert_ids.T, gate_prob.T)
    return pl.pallas_call(
        functools.partial(norm_body, expert_count),
        out_shape=pltpu.VMEM((rows, width + EXTRA), BF16),
        in_specs=[ANY_FULL] * 4,
        out_specs=VMEM_FULL,
        scratch_shapes=[pltpu.VMEM(v.shape, v.dtype) for v in args]
        + [pltpu.SemaphoreType.DMA((4,))],
        compiler_params=scoped,
    )(*[in_hbm(v) for v in args])


def fetch_body(ahead, order_ref, gate_hbm, up_hbm, gate_out, up_out, done_ref, sems):
    del order_ref
    copies = []
    for e in range(ahead):
        copies.append(pltpu.make_async_copy(gate_hbm.at[e], gate_out.at[e], sems.at[0, e]))
        copies.append(pltpu.make_async_copy(up_hbm.at[e], up_out.at[e], sems.at[1, e]))
    for copy in copies:
        copy.start()
    done_ref[...] = jnp.zeros_like(done_ref)
    for copy in copies:
        copy.wait()


def fetch_call(order, w_gate, w_up, scoped):
    local, width, hidden = w_gate.shape
    slots = min(SLOTS, local)
    ahead = min(AHEAD, local)
    return pl.pallas_call(
        functools.partial(fetch_body, ahead),
        out_shape=[pltpu.VMEM((slots, width, hidden), BF16)] * 2 + [pltpu.VMEM((8, 128), F32)],
        in_specs=[ANY_FULL] * 3,
        out_specs=[VMEM_FULL] * 3,
        scratch_shapes=[pltpu.SemaphoreType.DMA((2, slots))],
        compiler_params=scoped,
        cost_estimate=cost(0, 8 * slots * width * hidden),
    )(order, in_hbm(w_gate), in_hbm(w_up))


def gate_up_body(expert_count, parts, *refs):
    pieces, refs = refs[:parts], refs[parts:]
    gate_hbm, up_hbm, down_hbm = refs[2:5]
    out_ref, down_ref, gate_ref, up_ref, rows_ref, sems, down_sems = refs[5:]
    slots, width, hidden = gate_ref.shape
    local = gate_hbm.shape[0]
    ahead = min(AHEAD, slots)
    columns = down_ref.shape[1]

    def copies(e):
        slot = lax.rem(e, slots)
        return [
            pltpu.make_async_copy(gate_hbm.at[e], gate_ref.at[slot], sems.at[0, slot]),
            pltpu.make_async_copy(up_hbm.at[e], up_ref.at[slot], sems.at[1, slot]),
        ]

    def down_copy(e):
        at = pl.ds(pl.multiple_of(e * hidden, hidden), hidden)
        return pltpu.make_async_copy(down_hbm.at[at, :columns], down_ref.at[at], down_sems.at[e])

    for e in range(ahead, slots):
        for copy in copies(e):
            copy.start()
    for e in range(local):
        down_copy(e).start()
    at = 0
    for piece in pieces:
        rows_ref[at : at + piece.shape[0]] = piece[...]
        at += piece.shape[0]

    row = lax.broadcasted_iota(jnp.int32, (EXTRA, hidden), 0)
    number = lax.axis_index("exp") * local

    def one(e, carry):
        @pl.when((e >= 1) & (e <= local - slots))
        def _():
            for copy in copies(e - 1 + slots):
                copy.start()

        @pl.when(e >= ahead)
        def _():
            for copy in copies(e):
                copy.wait()

        slot = lax.rem(e, slots)
        weights = jnp.concatenate([gate_ref[slot], up_ref[slot]], axis=1)
        both = jnp.dot(rows_ref[:, :width], weights, preferred_element_type=F32)
        gate, up = both[:, :hidden], both[:, hidden:]
        pick = jnp.where((row % expert_count == number + e) & (row < 3 * expert_count), 1.0, 0.0)
        mixing = jnp.dot(rows_ref[:, width:], pick.astype(BF16), preferred_element_type=F32)
        value = gate / (1.0 + jnp.exp(-gate)) * up * mixing
        at = pl.ds(pl.multiple_of(e * hidden, hidden), hidden)
        out_ref[:, at] = value.astype(BF16)
        return carry

    lax.fori_loop(0, local, one, 0)
    for e in range(local):
        down_copy(e).wait()


def gate_up_call(pieces, gate_slots, up_slots, w_gate, w_up, w_down, expert_count, scoped):
    slots, width, hidden = gate_slots.shape
    local = w_gate.shape[0]
    depth = w_down.shape[0]
    rows = sum(p.shape[0] for p in pieces)
    count = len(pieces)
    shape = pltpu.VMEM(gate_slots.shape, BF16)
    return pl.pallas_call(
        functools.partial(gate_up_body, expert_count, count),
        out_shape=[pltpu.VMEM((rows, depth), BF16), pltpu.VMEM((depth, 3 * width // 4), BF16), shape, shape],
        in_specs=[VMEM_FULL] * (count + 2) + [ANY_FULL] * 3,
        out_specs=[VMEM_FULL] * 4,
        scratch_shapes=[
            pltpu.VMEM((rows, width + EXTRA), BF16),
            pltpu.SemaphoreType.DMA((2, slots)),
            pltpu.SemaphoreType.DMA((local,)),
        ],
        input_output_aliases={count: 2, count + 1: 3},
        compiler_params=scoped,
        cost_estimate=cost(4 * rows * width * hidden * local, 6 * width * hidden * local),
    )(
        *[in_vmem(v) for v in (*pieces, gate_slots, up_slots)],
        *[in_hbm(v) for v in (w_gate, w_up, w_down)],
    )[:2]


def down_body(half, start, more, hidden_ref, *refs):
    if more:
        weight_ref, down_hbm, keep_ref, send_ref, rest_ref, sems = refs
        parts = sems.shape[0]
        step = rest_ref.shape[0] // parts
        skip = down_hbm.shape[1] - rest_ref.shape[1]
        copies = []
        for i in range(parts):
            at = slice(i * step, (i + 1) * step)
            copies.append(
                pltpu.make_async_copy(down_hbm.at[at, skip:], rest_ref.at[at], sems.at[i])
            )
    else:
        weight_ref, rest_ref, keep_ref, send_ref = refs
        copies = []
    for copy in copies:
        copy.start()
    ready = weight_ref.shape[1]
    block = 512

    def run(ref, skip, first, stop):
        def one(i, carry):
            to = pl.ds(pl.multiple_of(i * block, block), block)
            at = pl.ds(pl.multiple_of(skip + i * block, block), block)
            out = jnp.dot(hidden_ref[...], ref[:, at], preferred_element_type=F32).astype(BF16)
            keep_ref[:, to] = out[:half]
            send_ref[:, to] = out[half:]
            return carry

        lax.fori_loop(first, stop, one, 0)

    stop = keep_ref.shape[1]
    middle = min(stop, ready - start)
    run(weight_ref, start, 0, middle // block)
    if middle < stop:
        run(rest_ref, start - ready, middle // block, stop // block)
    for copy in copies:
        copy.wait()


def down_call(start, step, hidden, weight, w_down, rest, scoped):
    rows, depth = hidden.shape
    half = rows // 2
    more = rest is None
    last = w_down.shape[1] - weight.shape[1]
    return pl.pallas_call(
        functools.partial(down_body, half, start, more),
        out_shape=[pltpu.VMEM((half, step), BF16)] * 2
        + ([pltpu.VMEM((depth, last), BF16)] if more else []),
        in_specs=[VMEM_FULL] * 2 + [ANY_FULL if more else VMEM_FULL],
        out_specs=[VMEM_FULL] * (3 if more else 2),
        scratch_shapes=[pltpu.SemaphoreType.DMA((8,))] if more else [],
        compiler_params=scoped,
        cost_estimate=cost(2 * rows * depth * step, 2 * depth * step),
    )(in_vmem(hidden), in_vmem(weight), in_hbm(w_down) if more else in_vmem(rest))


def pair_body(keep_ref, got_ref, *outs):
    rows = outs[0].shape[0]
    for k, out in enumerate(outs):
        at = slice(k * rows, (k + 1) * rows)
        out[...] = (keep_ref[at].astype(F32) + got_ref[at].astype(F32)).astype(BF16)


def pair_call(keep, got, rows, scoped):
    count = keep.shape[0] // rows
    return pl.pallas_call(
        pair_body,
        out_shape=[pltpu.VMEM((rows, keep.shape[1]), BF16)] * count,
        in_specs=[VMEM_FULL] * 2,
        out_specs=[VMEM_FULL] * count,
        compiler_params=scoped,
    )(in_vmem(keep), in_vmem(got))


def finish_body(chunks, *refs):
    ins, out_ref = refs[:-1], refs[-1]
    count = len(ins) // chunks
    step = ins[0].shape[1]
    for j in range(chunks):
        total = ins[j * count][...].astype(F32)
        for ref in ins[j * count + 1 : (j + 1) * count]:
            total = total + ref[...].astype(F32)
        out_ref[:, j * step : (j + 1) * step] = total.astype(BF16)


def finish_call(parts, chunks, rows, width, scoped):
    return pl.pallas_call(
        functools.partial(finish_body, chunks),
        out_shape=jax.ShapeDtypeStruct((rows, width), BF16),
        in_specs=[VMEM_FULL] * len(parts),
        out_specs=VMEM_FULL,
        compiler_params=scoped,
    )(*[in_vmem(p) for p in parts])


def per_device(tokens, norm_gain, expert_ids, gate_prob, w_gate, w_up, w_down):
    rows, width = tokens.shape
    local, _, hidden = w_gate.shape
    size = lax.axis_size("exp") * lax.axis_size("ten")
    expert_count = local * lax.axis_size("exp")
    far = range(2, size, 2)
    w_rows = w_down.reshape(local * hidden, width)

    scoped = params(size * rows, width)

    own = norm_call(tokens, norm_gain, expert_ids, gate_prob, expert_count, scoped)
    gate_slots, up_slots, fetched = fetch_call(own, w_gate, w_up, scoped)
    near = [own] + [after(exchange(own, size, mask), fetched) for mask in far]
    pieces = near + [exchange(piece, size, 1) for piece in near]
    mixed_hidden, weight = gate_up_call(
        pieces, gate_slots, up_slots, w_gate, w_up, w_rows, expert_count, scoped
    )
    step = width // 2
    keep_a, send_a, rest = down_call(0, step, mixed_hidden, weight, w_rows, None, scoped)
    keep_b, send_b = down_call(step, step, mixed_hidden, weight, w_rows, rest, scoped)
    parts = []
    for keep, send in ((keep_a, send_a), (keep_b, send_b)):
        blocks = pair_call(keep, exchange(send, size, 1), rows, scoped)
        parts += [exchange(b, size, mask) for b, mask in zip(blocks[:0:-1], far[::-1])]
        parts.append(blocks[0])
    return finish_call(parts, 2, rows, width, scoped)


def solution(mesh):
    placed = (
        P(("grp", "exp", "ten"), None),
        P(),
        P(("grp", "exp", "ten"), None),
        P(("grp", "exp", "ten"), None),
        P("exp", None, "ten"),
        P("exp", None, "ten"),
        P("exp", "ten", None),
    )
    return jax.shard_map(
        per_device,
        mesh=mesh,
        in_specs=placed,
        out_specs=P(("grp", "exp", "ten"), None),
        check_vma=False,
    )
```

```python
import functools

import jax
import jax.numpy as jnp
from jax import lax
from jax.experimental import pallas as pl
from jax.experimental.pallas import tpu as pltpu
from jax.sharding import PartitionSpec as P

BF16 = jnp.bfloat16
F32 = jnp.float32
MIB = 2**20
GROUP = ("exp", "ten")
EXTRA = 128
SLOTS = 5
AHEAD = 5
BLOCK = 1024
VMEM_FULL = pl.BlockSpec(memory_space=pltpu.VMEM)
ANY_FULL = pl.BlockSpec(memory_space=pl.ANY)


def in_vmem(value):
    return pltpu.with_memory_space_constraint(value, pltpu.VMEM)


def in_hbm(value):
    return pltpu.with_memory_space_constraint(value, pltpu.HBM)


def params(rows, width):
    return pltpu.CompilerParams(vmem_limit_bytes=2 * MIB + 4 * rows * width)


def cost(flops, read):
    return pl.CostEstimate(flops=flops, bytes_accessed=read, transcendentals=0)


def exchange(value, size, mask):
    return lax.ppermute(value, GROUP, [(i, i ^ mask) for i in range(size)])


def after(value, other):
    return lax.optimization_barrier((value, other))[0]


def norm_body(expert_count, *refs):
    sources, out_ref, targets, sems = refs[:4], refs[4], refs[5:9], refs[9]
    copies = [
        pltpu.make_async_copy(source, target, sems.at[i])
        for i, (source, target) in enumerate(zip(sources, targets))
    ]
    for copy in copies:
        copy.start()
    for copy in copies:
        copy.wait()
    tok_ref, gain_ref, ids_ref, prob_ref = targets
    width = tok_ref.shape[1]
    floats = tok_ref[...].astype(F32)
    meansq = jnp.mean(floats * floats, axis=1, keepdims=True)
    out_ref[:, :width] = (floats * lax.rsqrt(meansq + 1e-06) * gain_ref[...]).astype(BF16)
    prob = prob_ref[...]
    mixing = prob / jnp.sum(prob, axis=0, keepdims=True)
    place = lax.broadcasted_iota(jnp.int32, (EXTRA, prob.shape[1]), 0)
    weight = jnp.zeros(place.shape, F32)
    for k in range(prob.shape[0]):
        weight = weight + jnp.where(
            place % expert_count == ids_ref[k : k + 1], mixing[k : k + 1], 0.0
        )
    high = weight.astype(BF16).astype(F32)
    middle = (weight - high).astype(BF16).astype(F32)
    low = weight - high - middle
    piece = place // expert_count
    packed = jnp.where(piece == 0, high, jnp.where(piece == 1, middle, jnp.where(piece == 2, low, 0.0)))
    out_ref[:, width:] = packed.T.astype(BF16)


def norm_call(tokens, norm_gain, expert_ids, gate_prob, expert_count, scoped):
    rows, width = tokens.shape
    args = (tokens, norm_gain.reshape(1, width), expert_ids.T, gate_prob.T)
    return pl.pallas_call(
        functools.partial(norm_body, expert_count),
        out_shape=pltpu.VMEM((rows, width + EXTRA), BF16),
        in_specs=[ANY_FULL] * 4,
        out_specs=VMEM_FULL,
        scratch_shapes=[pltpu.VMEM(v.shape, v.dtype) for v in args]
        + [pltpu.SemaphoreType.DMA((4,))],
        compiler_params=scoped,
    )(*[in_hbm(v) for v in args])


def fetch_body(ahead, order_ref, gate_hbm, up_hbm, gate_out, up_out, done_ref, sems):
    del order_ref
    copies = []
    for e in range(ahead):
        copies.append(pltpu.make_async_copy(gate_hbm.at[e], gate_out.at[e], sems.at[0, e]))
        copies.append(pltpu.make_async_copy(up_hbm.at[e], up_out.at[e], sems.at[1, e]))
    for copy in copies:
        copy.start()
    done_ref[...] = jnp.zeros_like(done_ref)
    for copy in copies:
        copy.wait()


def fetch_call(order, w_gate, w_up, scoped):
    local, width, hidden = w_gate.shape
    slots = min(SLOTS, local)
    ahead = min(AHEAD, local)
    return pl.pallas_call(
        functools.partial(fetch_body, ahead),
        out_shape=[pltpu.VMEM((slots, width, hidden), BF16)] * 2 + [pltpu.VMEM((8, 128), F32)],
        in_specs=[ANY_FULL] * 3,
        out_specs=[VMEM_FULL] * 3,
        scratch_shapes=[pltpu.SemaphoreType.DMA((2, slots))],
        compiler_params=scoped,
        cost_estimate=cost(0, 8 * slots * width * hidden),
    )(order, in_hbm(w_gate), in_hbm(w_up))


def gate_up_body(expert_count, parts, *refs):
    pieces, refs = refs[:parts], refs[parts:]
    gate_hbm, up_hbm, down_hbm = refs[2:5]
    out_ref, down_ref, gate_ref, up_ref, rows_ref, sems, down_sems = refs[5:]
    slots, width, hidden = gate_ref.shape
    local = gate_hbm.shape[0]
    ahead = min(AHEAD, slots)
    columns = down_ref.shape[1]

    def copies(e):
        slot = lax.rem(e, slots)
        return [
            pltpu.make_async_copy(gate_hbm.at[e], gate_ref.at[slot], sems.at[0, slot]),
            pltpu.make_async_copy(up_hbm.at[e], up_ref.at[slot], sems.at[1, slot]),
        ]

    def down_copy(e):
        at = pl.ds(pl.multiple_of(e * hidden, hidden), hidden)
        return pltpu.make_async_copy(down_hbm.at[at, :columns], down_ref.at[at], down_sems.at[e])

    for e in range(ahead, slots):
        for copy in copies(e):
            copy.start()
    for e in range(local):
        down_copy(e).start()
    at = 0
    for piece in pieces:
        rows_ref[at : at + piece.shape[0]] = piece[...]
        at += piece.shape[0]

    row = lax.broadcasted_iota(jnp.int32, (EXTRA, hidden), 0)
    number = lax.axis_index("exp") * local

    def one(e, carry):
        @pl.when((e >= 1) & (e <= local - slots))
        def _():
            for copy in copies(e - 1 + slots):
                copy.start()

        @pl.when(e >= ahead)
        def _():
            for copy in copies(e):
                copy.wait()

        slot = lax.rem(e, slots)
        weights = jnp.concatenate([gate_ref[slot], up_ref[slot]], axis=1)
        both = jnp.dot(rows_ref[:, :width], weights, preferred_element_type=F32)
        gate, up = both[:, :hidden], both[:, hidden:]
        pick = jnp.where((row % expert_count == number + e) & (row < 3 * expert_count), 1.0, 0.0)
        mixing = jnp.dot(rows_ref[:, width:], pick.astype(BF16), preferred_element_type=F32)
        value = gate / (1.0 + jnp.exp(-gate)) * up * mixing
        at = pl.ds(pl.multiple_of(e * hidden, hidden), hidden)
        out_ref[:, at] = value.astype(BF16)
        return carry

    lax.fori_loop(0, local, one, 0)
    for e in range(local):
        down_copy(e).wait()


def gate_up_call(pieces, gate_slots, up_slots, w_gate, w_up, w_down, expert_count, scoped):
    slots, width, hidden = gate_slots.shape
    local = w_gate.shape[0]
    depth = w_down.shape[0]
    rows = sum(p.shape[0] for p in pieces)
    count = len(pieces)
    shape = pltpu.VMEM(gate_slots.shape, BF16)
    return pl.pallas_call(
        functools.partial(gate_up_body, expert_count, count),
        out_shape=[pltpu.VMEM((rows, depth), BF16), pltpu.VMEM((depth, 3 * width // 4), BF16), shape, shape],
        in_specs=[VMEM_FULL] * (count + 2) + [ANY_FULL] * 3,
        out_specs=[VMEM_FULL] * 4,
        scratch_shapes=[
            pltpu.VMEM((rows, width + EXTRA), BF16),
            pltpu.SemaphoreType.DMA((2, slots)),
            pltpu.SemaphoreType.DMA((local,)),
        ],
        input_output_aliases={count: 2, count + 1: 3},
        compiler_params=scoped,
        cost_estimate=cost(4 * rows * width * hidden * local, 6 * width * hidden * local),
    )(
        *[in_vmem(v) for v in (*pieces, gate_slots, up_slots)],
        *[in_hbm(v) for v in (w_gate, w_up, w_down)],
    )[:2]


def down_body(half, start, more, hidden_ref, *refs):
    if more:
        weight_ref, down_hbm, keep_ref, send_ref, rest_ref, sems = refs
        parts = sems.shape[0]
        step = rest_ref.shape[0] // parts
        skip = down_hbm.shape[1] - rest_ref.shape[1]
        copies = []
        for i in range(parts):
            at = slice(i * step, (i + 1) * step)
            copies.append(
                pltpu.make_async_copy(down_hbm.at[at, skip:], rest_ref.at[at], sems.at[i])
            )
    else:
        weight_ref, rest_ref, keep_ref, send_ref = refs
        copies = []
    for copy in copies:
        copy.start()
    ready = weight_ref.shape[1]

    def run(ref, skip, first, stop):
        block = BLOCK if (stop - first) % BLOCK == 0 else 512

        def one(i, carry):
            to = pl.ds(pl.multiple_of(first + i * block, 128), block)
            at = pl.ds(pl.multiple_of(skip + first + i * block, 128), block)
            out = jnp.dot(hidden_ref[...], ref[:, at], preferred_element_type=F32).astype(BF16)
            keep_ref[:, to] = out[:half]
            send_ref[:, to] = out[half:]
            return carry

        lax.fori_loop(0, (stop - first) // block, one, 0, unroll=not more)

    stop = keep_ref.shape[1]
    middle = min(stop, ready - start)
    run(weight_ref, start, 0, middle)
    if middle < stop:
        run(rest_ref, start - ready, middle, stop)
    for copy in copies:
        copy.wait()


def down_call(start, step, hidden, weight, w_down, rest, scoped):
    rows, depth = hidden.shape
    half = rows // 2
    more = rest is None
    last = w_down.shape[1] - weight.shape[1]
    return pl.pallas_call(
        functools.partial(down_body, half, start, more),
        out_shape=[pltpu.VMEM((half, step), BF16)] * 2
        + ([pltpu.VMEM((depth, last), BF16)] if more else []),
        in_specs=[VMEM_FULL] * 2 + [ANY_FULL if more else VMEM_FULL],
        out_specs=[VMEM_FULL] * (3 if more else 2),
        scratch_shapes=[pltpu.SemaphoreType.DMA((8,))] if more else [],
        compiler_params=scoped,
        cost_estimate=cost(2 * rows * depth * step, 2 * depth * step),
    )(in_vmem(hidden), in_vmem(weight), in_hbm(w_down) if more else in_vmem(rest))


def pair_body(keep_ref, got_ref, *outs):
    rows = outs[0].shape[0]
    for k, out in enumerate(outs):
        at = slice(k * rows, (k + 1) * rows)
        out[...] = (keep_ref[at].astype(F32) + got_ref[at].astype(F32)).astype(BF16)


def pair_call(keep, got, rows, scoped):
    count = keep.shape[0] // rows
    return pl.pallas_call(
        pair_body,
        out_shape=[pltpu.VMEM((rows, keep.shape[1]), BF16)] * count,
        in_specs=[VMEM_FULL] * 2,
        out_specs=[VMEM_FULL] * count,
        compiler_params=scoped,
    )(in_vmem(keep), in_vmem(got))


def add_body(left_ref, right_ref, out_ref):
    out_ref[...] = (left_ref[...].astype(F32) + right_ref[...].astype(F32)).astype(BF16)


def add_call(left, right, scoped):
    return pl.pallas_call(
        add_body,
        out_shape=pltpu.VMEM(left.shape, BF16),
        in_specs=[VMEM_FULL] * 2,
        out_specs=VMEM_FULL,
        compiler_params=scoped,
    )(in_vmem(left), in_vmem(right))


def finish_body(counts, *refs):
    ins, out_ref = refs[:-1], refs[-1]
    start = 0
    for count in counts:
        terms, ins = ins[:count], ins[count:]
        stop = start + terms[0].shape[1]
        total = terms[0][...].astype(F32)
        for ref in terms[1:]:
            total = total + ref[...].astype(F32)
        out_ref[:, start:stop] = total.astype(BF16)
        start = stop


def finish_call(chunks, rows, width, scoped):
    parts = [p for chunk in chunks for p in chunk]
    return pl.pallas_call(
        functools.partial(finish_body, [len(chunk) for chunk in chunks]),
        out_shape=jax.ShapeDtypeStruct((rows, width), BF16),
        in_specs=[VMEM_FULL] * len(parts),
        out_specs=VMEM_FULL,
        compiler_params=scoped,
    )(*[in_vmem(p) for p in parts])


def per_device(tokens, norm_gain, expert_ids, gate_prob, w_gate, w_up, w_down):
    rows, width = tokens.shape
    local, _, hidden = w_gate.shape
    size = lax.axis_size("exp") * lax.axis_size("ten")
    expert_count = local * lax.axis_size("exp")
    far = range(2, size, 2)
    w_rows = w_down.reshape(local * hidden, width)

    scoped = params(size * rows, width)

    own = norm_call(tokens, norm_gain, expert_ids, gate_prob, expert_count, scoped)
    gate_slots, up_slots, fetched = fetch_call(own, w_gate, w_up, scoped)
    near = [own] + [after(exchange(own, size, mask), fetched) for mask in far]
    pieces = near + [exchange(piece, size, 1) for piece in near]
    mixed_hidden, weight = gate_up_call(
        pieces, gate_slots, up_slots, w_gate, w_up, w_rows, expert_count, scoped
    )
    step = width // 2
    keep_a, send_a, rest = down_call(0, step, mixed_hidden, weight, w_rows, None, scoped)
    keep_b, send_b = down_call(step, width - step, mixed_hidden, weight, w_rows, rest, scoped)
    got_a, got_b = exchange(send_a, size, 1), exchange(send_b, size, 1)
    blocks_a = pair_call(keep_a, got_a, rows, scoped)
    blocks_b = pair_call(keep_b, got_b, rows, scoped)
    if len(blocks_a) != 4:
        chunks = []
        for blocks in (blocks_a, blocks_b):
            sent = [exchange(b, size, mask) for b, mask in zip(blocks[1:], far)]
            chunks.append([blocks[0], *sent])
        return finish_call(chunks, rows, width, scoped)

    def over(block, axis):
        return exchange(block, size, far[axis])

    own_a, first_a, second_a, both_a = blocks_a
    own_b, first_b, second_b, both_b = blocks_b
    passed_a = over(both_a, 1)
    direct_a = over(second_a, 1)
    passed_b = over(both_b, 0)
    direct_b = over(first_b, 0)
    summed_a = over(add_call(first_a, passed_a, scoped), 0)
    summed_b = over(add_call(second_b, passed_b, scoped), 1)
    chunks = [[own_a, direct_a, summed_a], [own_b, direct_b, summed_b]]
    return finish_call(chunks, rows, width, scoped)


def solution(mesh):
    placed = (
        P(("grp", "exp", "ten"), None),
        P(),
        P(("grp", "exp", "ten"), None),
        P(("grp", "exp", "ten"), None),
        P("exp", None, "ten"),
        P("exp", None, "ten"),
        P("exp", "ten", None),
    )
    return jax.shard_map(
        per_device,
        mesh=mesh,
        in_specs=placed,
        out_specs=P(("grp", "exp", "ten"), None),
        check_vma=False,
    )
```

```python
import functools

import jax
import jax.numpy as jnp
from jax import lax
from jax.experimental import pallas as pl
from jax.experimental.pallas import tpu as pltpu
from jax.sharding import PartitionSpec as P

BF16 = jnp.bfloat16
F32 = jnp.float32
MIB = 2**20
GROUP = ("exp", "ten")
EXTRA = 128
SLOTS = 6
AHEAD = 5
BLOCK = 1024
VMEM_FULL = pl.BlockSpec(memory_space=pltpu.VMEM)
ANY_FULL = pl.BlockSpec(memory_space=pl.ANY)


def in_vmem(value):
    return pltpu.with_memory_space_constraint(value, pltpu.VMEM)


def in_hbm(value):
    return pltpu.with_memory_space_constraint(value, pltpu.HBM)


def params(rows, width):
    return pltpu.CompilerParams(vmem_limit_bytes=2 * MIB + 4 * rows * width)


def cost(flops, read):
    return pl.CostEstimate(flops=flops, bytes_accessed=read, transcendentals=0)


def exchange(value, size, mask):
    return lax.ppermute(value, GROUP, [(i, i ^ mask) for i in range(size)])


def after(value, other):
    return lax.optimization_barrier((value, other))[0]


def norm_body(expert_count, *refs):
    sources, out_ref, targets, sems = refs[:4], refs[4], refs[5:9], refs[9]
    copies = [
        pltpu.make_async_copy(source, target, sems.at[i])
        for i, (source, target) in enumerate(zip(sources, targets))
    ]
    for copy in copies:
        copy.start()
    for copy in copies:
        copy.wait()
    tok_ref, gain_ref, ids_ref, prob_ref = targets
    width = tok_ref.shape[1]
    floats = tok_ref[...].astype(F32)
    meansq = jnp.mean(floats * floats, axis=1, keepdims=True)
    out_ref[:, :width] = (floats * lax.rsqrt(meansq + 1e-06) * gain_ref[...]).astype(BF16)
    prob = prob_ref[...]
    mixing = prob / jnp.sum(prob, axis=0, keepdims=True)
    place = lax.broadcasted_iota(jnp.int32, (EXTRA, prob.shape[1]), 0)
    weight = jnp.zeros(place.shape, F32)
    for k in range(prob.shape[0]):
        weight = weight + jnp.where(
            place % expert_count == ids_ref[k : k + 1], mixing[k : k + 1], 0.0
        )
    high = weight.astype(BF16).astype(F32)
    middle = (weight - high).astype(BF16).astype(F32)
    low = weight - high - middle
    piece = place // expert_count
    packed = jnp.where(piece == 0, high, jnp.where(piece == 1, middle, jnp.where(piece == 2, low, 0.0)))
    out_ref[:, width:] = packed.T.astype(BF16)


def norm_call(tokens, norm_gain, expert_ids, gate_prob, expert_count, scoped):
    rows, width = tokens.shape
    args = (tokens, norm_gain.reshape(1, width), expert_ids.T, gate_prob.T)
    return pl.pallas_call(
        functools.partial(norm_body, expert_count),
        out_shape=pltpu.VMEM((rows, width + EXTRA), BF16),
        in_specs=[ANY_FULL] * 4,
        out_specs=VMEM_FULL,
        scratch_shapes=[pltpu.VMEM(v.shape, v.dtype) for v in args]
        + [pltpu.SemaphoreType.DMA((4,))],
        compiler_params=scoped,
    )(*[in_hbm(v) for v in args])


def assemble(pieces, rows_ref):
    at = 0
    for piece in pieces:
        rows_ref[at : at + piece.shape[0]] = piece[...]
        at += piece.shape[0]


def hidden_of(rows_ref, first, gate_weight, up_weight, expert, expert_count):
    width, hidden = gate_weight.shape
    weights = jnp.concatenate([gate_weight, up_weight], axis=1)
    both = jnp.dot(rows_ref[first:, :width], weights, preferred_element_type=F32)
    gate, up = both[:, :hidden], both[:, hidden:]
    row = lax.broadcasted_iota(jnp.int32, (EXTRA, hidden), 0)
    pick = jnp.where((row % expert_count == expert) & (row < 3 * expert_count), 1.0, 0.0)
    mixing = jnp.dot(rows_ref[first:, width:], pick.astype(BF16), preferred_element_type=F32)
    return (gate / (1.0 + jnp.exp(-gate)) * up * mixing).astype(BF16)


def fetch_body(ahead, expert_count, parts, *refs):
    pieces, refs = refs[:parts], refs[parts:]
    gate_hbm, up_hbm, gate_ref, up_ref, early_ref, done_ref, rows_ref, sems = refs
    local, _, hidden = gate_hbm.shape

    def copies(e):
        return [
            pltpu.make_async_copy(gate_hbm.at[e], gate_ref.at[e], sems.at[0, e]),
            pltpu.make_async_copy(up_hbm.at[e], up_ref.at[e], sems.at[1, e]),
        ]

    for e in range(ahead):
        for copy in copies(e):
            copy.start()
    done_ref[...] = jnp.zeros_like(done_ref)
    assemble(pieces, rows_ref)
    number = lax.axis_index("exp") * local

    def one(e, carry):
        for copy in copies(e):
            copy.wait()
        at = pl.ds(pl.multiple_of(e * hidden, hidden), hidden)
        early_ref[:, at] = hidden_of(
            rows_ref, 0, gate_ref[e], up_ref[e], number + e, expert_count
        )
        return carry

    lax.fori_loop(0, ahead, one, 0)


def fetch_call(pieces, w_gate, w_up, expert_count, scoped):
    local, width, hidden = w_gate.shape
    slots, ahead = min(SLOTS, local), min(AHEAD, local)
    rows = sum(p.shape[0] for p in pieces)
    return pl.pallas_call(
        functools.partial(fetch_body, ahead, expert_count, len(pieces)),
        out_shape=[pltpu.VMEM((slots, width, hidden), BF16)] * 2
        + [pltpu.VMEM((rows, ahead * hidden), BF16), pltpu.VMEM((8, 128), F32)],
        in_specs=[VMEM_FULL] * len(pieces) + [ANY_FULL] * 2,
        out_specs=[VMEM_FULL] * 4,
        scratch_shapes=[
            pltpu.VMEM((rows, width + EXTRA), BF16),
            pltpu.SemaphoreType.DMA((2, ahead)),
        ],
        compiler_params=scoped,
        cost_estimate=cost(0, 8 * ahead * width * hidden),
    )(*[in_vmem(p) for p in pieces], in_hbm(w_gate), in_hbm(w_up))


def gate_up_body(expert_count, parts, *refs):
    pieces, refs = refs[:parts], refs[parts:]
    early_ref, gate_hbm, up_hbm, down_hbm = refs[0], *refs[3:6]
    out_ref, down_ref, gate_ref, up_ref, rows_ref, sems, down_sems = refs[6:]
    slots, width, hidden = gate_ref.shape
    local = gate_hbm.shape[0]
    ahead = min(AHEAD, slots)
    columns = down_ref.shape[1]
    first, ready = early_ref.shape

    def copies(e):
        slot = lax.rem(e, slots)
        return [
            pltpu.make_async_copy(gate_hbm.at[e], gate_ref.at[slot], sems.at[0, slot]),
            pltpu.make_async_copy(up_hbm.at[e], up_ref.at[slot], sems.at[1, slot]),
        ]

    def down_copy(e):
        at = pl.ds(pl.multiple_of(e * hidden, hidden), hidden)
        return pltpu.make_async_copy(down_hbm.at[at, :columns], down_ref.at[at], down_sems.at[e])

    for e in range(ahead, slots):
        for copy in copies(e):
            copy.start()
    for e in range(local):
        down_copy(e).start()
    assemble(pieces, rows_ref)
    out_ref[:first, :ready] = early_ref[...]
    number = lax.axis_index("exp") * local

    def run(skip, e, carry):
        @pl.when((e >= 1) & (e <= local - slots))
        def _():
            for copy in copies(e - 1 + slots):
                copy.start()

        @pl.when(e >= ahead)
        def _():
            for copy in copies(e):
                copy.wait()

        slot = lax.rem(e, slots)
        at = pl.ds(pl.multiple_of(e * hidden, hidden), hidden)
        out_ref[skip:, at] = hidden_of(
            rows_ref, skip, gate_ref[slot], up_ref[slot], number + e, expert_count
        )
        return carry

    lax.fori_loop(0, ready // hidden, functools.partial(run, first), 0)
    lax.fori_loop(ready // hidden, local, functools.partial(run, 0), 0)
    for e in range(local):
        down_copy(e).wait()


def gate_up_call(pieces, early, gate_slots, up_slots, w_gate, w_up, w_down, expert_count, scoped):
    slots, width, hidden = gate_slots.shape
    local = w_gate.shape[0]
    depth = w_down.shape[0]
    rows = sum(p.shape[0] for p in pieces)
    count = len(pieces)
    shape = pltpu.VMEM(gate_slots.shape, BF16)
    return pl.pallas_call(
        functools.partial(gate_up_body, expert_count, count),
        out_shape=[pltpu.VMEM((rows, depth), BF16), pltpu.VMEM((depth, 5 * width // 8), BF16), shape, shape],
        in_specs=[VMEM_FULL] * (count + 3) + [ANY_FULL] * 3,
        out_specs=[VMEM_FULL] * 4,
        scratch_shapes=[
            pltpu.VMEM((rows, width + EXTRA), BF16),
            pltpu.SemaphoreType.DMA((2, slots)),
            pltpu.SemaphoreType.DMA((local,)),
        ],
        input_output_aliases={count + 1: 2, count + 2: 3},
        compiler_params=scoped,
        cost_estimate=cost(4 * rows * width * hidden * local, 6 * width * hidden * local),
    )(
        *[in_vmem(v) for v in (*pieces, early, gate_slots, up_slots)],
        *[in_hbm(v) for v in (w_gate, w_up, w_down)],
    )[:2]


def down_body(order, rows, start, more, hidden_ref, *refs):
    if more:
        weight_ref, down_hbm, keep_ref, send_ref, rest_ref, sems = refs
        parts = sems.shape[0]
        step = rest_ref.shape[0] // parts
        skip = down_hbm.shape[1] - rest_ref.shape[1]
        copies = []
        for i in range(parts):
            at = slice(i * step, (i + 1) * step)
            copies.append(
                pltpu.make_async_copy(down_hbm.at[at, skip:], rest_ref.at[at], sems.at[i])
            )
    else:
        weight_ref, rest_ref, keep_ref, send_ref = refs
        copies = []
    for copy in copies:
        copy.start()
    ready = weight_ref.shape[1]

    def run(ref, skip, first, stop):
        block = BLOCK if (stop - first) % BLOCK == 0 else 512

        def one(i, carry):
            to = pl.ds(pl.multiple_of(first + i * block, 128), block)
            at = pl.ds(pl.multiple_of(skip + first + i * block, 128), block)
            out = jnp.dot(hidden_ref[...], ref[:, at], preferred_element_type=F32).astype(BF16)
            for k, (near, other) in enumerate(order):
                block_rows = slice(k * rows, (k + 1) * rows)
                keep_ref[block_rows, to] = out[near * rows : (near + 1) * rows]
                send_ref[block_rows, to] = out[other * rows : (other + 1) * rows]
            return carry

        lax.fori_loop(0, (stop - first) // block, one, 0, unroll=not more)

    stop = keep_ref.shape[1]
    middle = min(stop, ready - start)
    run(weight_ref, start, 0, middle)
    if middle < stop:
        run(rest_ref, start - ready, middle, stop)
    for copy in copies:
        copy.wait()


def down_call(start, step, hidden, weight, w_down, rest, order, scoped):
    rows, depth = hidden.shape
    half = rows // 2
    block = half // len(order)
    more = rest is None
    last = w_down.shape[1] - weight.shape[1]
    return pl.pallas_call(
        functools.partial(down_body, order, block, start, more),
        out_shape=[pltpu.VMEM((half, step), BF16)] * 2
        + ([pltpu.VMEM((depth, last), BF16)] if more else []),
        in_specs=[VMEM_FULL] * 2 + [ANY_FULL if more else VMEM_FULL],
        out_specs=[VMEM_FULL] * (3 if more else 2),
        scratch_shapes=[pltpu.SemaphoreType.DMA((8,))] if more else [],
        compiler_params=scoped,
        cost_estimate=cost(2 * rows * depth * step, 2 * depth * step),
    )(in_vmem(hidden), in_vmem(weight), in_hbm(w_down) if more else in_vmem(rest))


def pair_body(keep_ref, got_ref, *outs):
    rows = outs[0].shape[0]
    for k, out in enumerate(outs):
        at = slice(k * rows, (k + 1) * rows)
        out[...] = (keep_ref[at].astype(F32) + got_ref[at].astype(F32)).astype(BF16)


def pair_call(keep, got, rows, scoped):
    count = keep.shape[0] // rows
    return pl.pallas_call(
        pair_body,
        out_shape=[pltpu.VMEM((rows, keep.shape[1]), BF16)] * count,
        in_specs=[VMEM_FULL] * 2,
        out_specs=[VMEM_FULL] * count,
        compiler_params=scoped,
    )(in_vmem(keep), in_vmem(got))


def add_body(left_ref, right_ref, out_ref):
    out_ref[...] = (left_ref[...].astype(F32) + right_ref[...].astype(F32)).astype(BF16)


def add_call(left, right, scoped):
    return pl.pallas_call(
        add_body,
        out_shape=pltpu.VMEM(left.shape, BF16),
        in_specs=[VMEM_FULL] * 2,
        out_specs=VMEM_FULL,
        compiler_params=scoped,
    )(in_vmem(left), in_vmem(right))


def finish_body(counts, *refs):
    ins, out_ref = refs[:-1], refs[-1]
    start = 0
    for count in counts:
        terms, ins = ins[:count], ins[count:]
        stop = start + terms[0].shape[1]
        total = terms[0][...].astype(F32)
        for ref in terms[1:]:
            total = total + ref[...].astype(F32)
        out_ref[:, start:stop] = total.astype(BF16)
        start = stop


def finish_call(chunks, rows, width, scoped):
    parts = [p for chunk in chunks for p in chunk]
    return pl.pallas_call(
        functools.partial(finish_body, [len(chunk) for chunk in chunks]),
        out_shape=jax.ShapeDtypeStruct((rows, width), BF16),
        in_specs=[VMEM_FULL] * len(parts),
        out_specs=VMEM_FULL,
        compiler_params=scoped,
    )(*[in_vmem(p) for p in parts])


def per_device(tokens, norm_gain, expert_ids, gate_prob, w_gate, w_up, w_down):
    rows, width = tokens.shape
    local, _, hidden = w_gate.shape
    size = lax.axis_size("exp") * lax.axis_size("ten")
    expert_count = local * lax.axis_size("exp")
    far = range(2, size, 2)
    w_rows = w_down.reshape(local * hidden, width)

    scoped = params(size * rows, width)

    own = norm_call(tokens, norm_gain, expert_ids, gate_prob, expert_count, scoped)
    ours = [own, exchange(own, size, 1)]
    *slots, early, fetched = fetch_call(ours, w_gate, w_up, expert_count, scoped)
    near = [after(exchange(own, size, mask), fetched) for mask in far]
    pieces = ours + near + [exchange(piece, size, 1) for piece in near]
    order = [(0, 1)] + [(2 + i, 2 + len(far) + i) for i in range(len(far))]
    mixed_hidden, weight = gate_up_call(
        pieces, early, *slots, w_gate, w_up, w_rows, expert_count, scoped
    )
    step = width // 2
    keep_a, send_a, rest = down_call(0, step, mixed_hidden, weight, w_rows, None, order, scoped)
    keep_b, send_b = down_call(step, width - step, mixed_hidden, weight, w_rows, rest, order, scoped)
    got_a, got_b = exchange(send_a, size, 1), exchange(send_b, size, 1)
    blocks_a = pair_call(keep_a, got_a, rows, scoped)
    blocks_b = pair_call(keep_b, got_b, rows, scoped)
    if len(blocks_a) != 4:
        chunks = []
        for blocks in (blocks_a, blocks_b):
            sent = [exchange(b, size, mask) for b, mask in zip(blocks[1:], far)]
            chunks.append([blocks[0], *sent])
        return finish_call(chunks, rows, width, scoped)

    def over(block, axis):
        return exchange(block, size, far[axis])

    own_a, first_a, second_a, both_a = blocks_a
    own_b, first_b, second_b, both_b = blocks_b
    passed_a = over(both_a, 1)
    direct_a = over(second_a, 1)
    passed_b = over(both_b, 0)
    direct_b = over(first_b, 0)
    summed_a = over(add_call(first_a, passed_a, scoped), 0)
    summed_b = over(add_call(second_b, passed_b, scoped), 1)
    chunks = [[own_a, direct_a, summed_a], [own_b, direct_b, summed_b]]
    return finish_call(chunks, rows, width, scoped)


def solution(mesh):
    placed = (
        P(("grp", "exp", "ten"), None),
        P(),
        P(("grp", "exp", "ten"), None),
        P(("grp", "exp", "ten"), None),
        P("exp", None, "ten"),
        P("exp", None, "ten"),
        P("exp", "ten", None),
    )
    return jax.shard_map(
        per_device,
        mesh=mesh,
        in_specs=placed,
        out_specs=P(("grp", "exp", "ten"), None),
        check_vma=False,
    )
```

```python
import functools

import jax
import jax.numpy as jnp
from jax import lax
from jax.experimental import pallas as pl
from jax.experimental.pallas import tpu as pltpu
from jax.sharding import PartitionSpec as P

BF16 = jnp.bfloat16
F32 = jnp.float32
MIB = 2**20
GROUP = ("exp", "ten")
EXTRA = 128
SLOTS = 6
AHEAD = 5
BLOCK = 1024
VMEM_FULL = pl.BlockSpec(memory_space=pltpu.VMEM)
ANY_FULL = pl.BlockSpec(memory_space=pl.ANY)


def in_vmem(value):
    return pltpu.with_memory_space_constraint(value, pltpu.VMEM)


def in_hbm(value):
    return pltpu.with_memory_space_constraint(value, pltpu.HBM)


def params(rows, width):
    return pltpu.CompilerParams(vmem_limit_bytes=2 * MIB + 4 * rows * width)


def cost(flops, read):
    return pl.CostEstimate(flops=flops, bytes_accessed=read, transcendentals=0)


def exchange(value, size, mask):
    return lax.ppermute(value, GROUP, [(i, i ^ mask) for i in range(size)])


def after(value, other):
    return lax.optimization_barrier((value, other))[0]


def norm_body(expert_count, *refs):
    sources, out_ref, targets, sems = refs[:4], refs[4], refs[5:9], refs[9]
    copies = [
        pltpu.make_async_copy(source, target, sems.at[i])
        for i, (source, target) in enumerate(zip(sources, targets))
    ]
    for copy in copies:
        copy.start()
    for copy in copies:
        copy.wait()
    tok_ref, gain_ref, ids_ref, prob_ref = targets
    width = tok_ref.shape[1]
    floats = tok_ref[...].astype(F32)
    meansq = jnp.mean(floats * floats, axis=1, keepdims=True)
    out_ref[:, :width] = (floats * lax.rsqrt(meansq + 1e-06) * gain_ref[...]).astype(BF16)
    prob = prob_ref[...]
    mixing = prob / jnp.sum(prob, axis=0, keepdims=True)
    place = lax.broadcasted_iota(jnp.int32, (EXTRA, prob.shape[1]), 0)
    weight = jnp.zeros(place.shape, F32)
    for k in range(prob.shape[0]):
        weight = weight + jnp.where(
            place % expert_count == ids_ref[k : k + 1], mixing[k : k + 1], 0.0
        )
    high = weight.astype(BF16).astype(F32)
    middle = (weight - high).astype(BF16).astype(F32)
    low = weight - high - middle
    piece = place // expert_count
    packed = jnp.where(piece == 0, high, jnp.where(piece == 1, middle, jnp.where(piece == 2, low, 0.0)))
    out_ref[:, width:] = packed.T.astype(BF16)


def norm_call(tokens, norm_gain, expert_ids, gate_prob, expert_count, scoped):
    rows, width = tokens.shape
    args = (tokens, norm_gain.reshape(1, width), expert_ids.T, gate_prob.T)
    return pl.pallas_call(
        functools.partial(norm_body, expert_count),
        out_shape=pltpu.VMEM((rows, width + EXTRA), BF16),
        in_specs=[ANY_FULL] * 4,
        out_specs=VMEM_FULL,
        scratch_shapes=[pltpu.VMEM(v.shape, v.dtype) for v in args]
        + [pltpu.SemaphoreType.DMA((4,))],
        compiler_params=scoped,
    )(*[in_hbm(v) for v in args])


def assemble(pieces, rows_ref):
    at = 0
    for piece in pieces:
        rows_ref[at : at + piece.shape[0]] = piece[...]
        at += piece.shape[0]


def hidden_of(rows_ref, first, gate_weight, up_weight, expert, expert_count):
    width, hidden = gate_weight.shape
    weights = jnp.concatenate([gate_weight, up_weight], axis=1)
    both = jnp.dot(rows_ref[first:, :width], weights, preferred_element_type=F32)
    gate, up = both[:, :hidden], both[:, hidden:]
    row = lax.broadcasted_iota(jnp.int32, (EXTRA, hidden), 0)
    pick = jnp.where((row % expert_count == expert) & (row < 3 * expert_count), 1.0, 0.0)
    mixing = jnp.dot(rows_ref[first:, width:], pick.astype(BF16), preferred_element_type=F32)
    return (gate / (1.0 + jnp.exp(-gate)) * up * mixing).astype(BF16)


def fetch_body(ahead, expert_count, parts, *refs):
    pieces, refs = refs[:parts], refs[parts:]
    gate_hbm, up_hbm, gate_ref, up_ref, early_ref, done_ref, rows_ref, sems = refs
    local, _, hidden = gate_hbm.shape

    def copies(e):
        return [
            pltpu.make_async_copy(gate_hbm.at[e], gate_ref.at[e], sems.at[0, e]),
            pltpu.make_async_copy(up_hbm.at[e], up_ref.at[e], sems.at[1, e]),
        ]

    for e in range(ahead):
        for copy in copies(e):
            copy.start()
    done_ref[...] = jnp.zeros_like(done_ref)
    assemble(pieces, rows_ref)
    number = lax.axis_index("exp") * local

    def one(e, carry):
        for copy in copies(e):
            copy.wait()
        at = pl.ds(pl.multiple_of(e * hidden, hidden), hidden)
        early_ref[:, at] = hidden_of(
            rows_ref, 0, gate_ref[e], up_ref[e], number + e, expert_count
        )
        return carry

    lax.fori_loop(0, ahead, one, 0)


def fetch_call(pieces, w_gate, w_up, expert_count, scoped):
    local, width, hidden = w_gate.shape
    slots, ahead = min(SLOTS, local), min(AHEAD, local)
    rows = sum(p.shape[0] for p in pieces)
    return pl.pallas_call(
        functools.partial(fetch_body, ahead, expert_count, len(pieces)),
        out_shape=[pltpu.VMEM((slots, width, hidden), BF16)] * 2
        + [pltpu.VMEM((rows, ahead * hidden), BF16), pltpu.VMEM((8, 128), F32)],
        in_specs=[VMEM_FULL] * len(pieces) + [ANY_FULL] * 2,
        out_specs=[VMEM_FULL] * 4,
        scratch_shapes=[
            pltpu.VMEM((rows, width + EXTRA), BF16),
            pltpu.SemaphoreType.DMA((2, ahead)),
        ],
        compiler_params=scoped,
        cost_estimate=cost(0, 8 * ahead * width * hidden),
    )(*[in_vmem(p) for p in pieces], in_hbm(w_gate), in_hbm(w_up))


def gate_up_body(expert_count, parts, *refs):
    pieces, refs = refs[:parts], refs[parts:]
    early_ref, gate_hbm, up_hbm, down_hbm = refs[0], *refs[3:6]
    out_ref, down_ref, gate_ref, up_ref, rows_ref, sems, down_sems = refs[6:]
    slots, width, hidden = gate_ref.shape
    local = gate_hbm.shape[0]
    ahead = min(AHEAD, slots)
    columns = down_ref.shape[1]
    first, ready = early_ref.shape

    def copies(e):
        slot = lax.rem(e, slots)
        return [
            pltpu.make_async_copy(gate_hbm.at[e], gate_ref.at[slot], sems.at[0, slot]),
            pltpu.make_async_copy(up_hbm.at[e], up_ref.at[slot], sems.at[1, slot]),
        ]

    def down_copy(e):
        at = pl.ds(pl.multiple_of(e * hidden, hidden), hidden)
        return pltpu.make_async_copy(down_hbm.at[at, :columns], down_ref.at[at], down_sems.at[e])

    for e in range(ahead, slots):
        for copy in copies(e):
            copy.start()
    assemble(pieces, rows_ref)
    out_ref[:first, :ready] = early_ref[...]
    number = lax.axis_index("exp") * local

    def run(skip, e, carry):
        @pl.when((e >= 1) & (e <= local - slots))
        def _():
            for copy in copies(e - 1 + slots):
                copy.start()

        @pl.when(e == local - slots)
        def _():
            for k in range(local):
                down_copy(k).start()

        @pl.when(e >= ahead)
        def _():
            for copy in copies(e):
                copy.wait()

        slot = lax.rem(e, slots)
        at = pl.ds(pl.multiple_of(e * hidden, hidden), hidden)
        out_ref[skip:, at] = hidden_of(
            rows_ref, skip, gate_ref[slot], up_ref[slot], number + e, expert_count
        )
        return carry

    lax.fori_loop(0, ready // hidden, functools.partial(run, first), 0)
    lax.fori_loop(ready // hidden, local, functools.partial(run, 0), 0)
    for e in range(local):
        down_copy(e).wait()


def gate_up_call(pieces, early, gate_slots, up_slots, w_gate, w_up, w_down, expert_count, scoped):
    slots, width, hidden = gate_slots.shape
    local = w_gate.shape[0]
    depth = w_down.shape[0]
    rows = sum(p.shape[0] for p in pieces)
    count = len(pieces)
    shape = pltpu.VMEM(gate_slots.shape, BF16)
    return pl.pallas_call(
        functools.partial(gate_up_body, expert_count, count),
        out_shape=[pltpu.VMEM((rows, depth), BF16), pltpu.VMEM((depth, 5 * width // 8), BF16), shape, shape],
        in_specs=[VMEM_FULL] * (count + 3) + [ANY_FULL] * 3,
        out_specs=[VMEM_FULL] * 4,
        scratch_shapes=[
            pltpu.VMEM((rows, width + EXTRA), BF16),
            pltpu.SemaphoreType.DMA((2, slots)),
            pltpu.SemaphoreType.DMA((local,)),
        ],
        input_output_aliases={count + 1: 2, count + 2: 3},
        compiler_params=scoped,
        cost_estimate=cost(4 * rows * width * hidden * local, 6 * width * hidden * local),
    )(
        *[in_vmem(v) for v in (*pieces, early, gate_slots, up_slots)],
        *[in_hbm(v) for v in (w_gate, w_up, w_down)],
    )[:2]


def down_body(order, rows, start, more, hidden_ref, *refs):
    if more:
        weight_ref, down_hbm, keep_ref, send_ref, rest_ref, sems = refs
        parts = sems.shape[0]
        step = rest_ref.shape[0] // parts
        skip = down_hbm.shape[1] - rest_ref.shape[1]
        copies = []
        for i in range(parts):
            at = slice(i * step, (i + 1) * step)
            copies.append(
                pltpu.make_async_copy(down_hbm.at[at, skip:], rest_ref.at[at], sems.at[i])
            )
    else:
        weight_ref, rest_ref, keep_ref, send_ref = refs
        copies = []
    for copy in copies:
        copy.start()
    ready = weight_ref.shape[1]

    def run(ref, skip, first, stop):
        block = BLOCK if (stop - first) % BLOCK == 0 else 512

        def one(i, carry):
            to = pl.ds(pl.multiple_of(first + i * block, 128), block)
            at = pl.ds(pl.multiple_of(skip + first + i * block, 128), block)
            out = jnp.dot(hidden_ref[...], ref[:, at], preferred_element_type=F32).astype(BF16)
            for k, (near, other) in enumerate(order):
                block_rows = slice(k * rows, (k + 1) * rows)
                keep_ref[block_rows, to] = out[near * rows : (near + 1) * rows]
                send_ref[block_rows, to] = out[other * rows : (other + 1) * rows]
            return carry

        lax.fori_loop(0, (stop - first) // block, one, 0, unroll=not more)

    stop = keep_ref.shape[1]
    middle = min(stop, ready - start)
    run(weight_ref, start, 0, middle)
    if middle < stop:
        run(rest_ref, start - ready, middle, stop)
    for copy in copies:
        copy.wait()


def down_call(start, step, hidden, weight, w_down, rest, order, scoped):
    rows, depth = hidden.shape
    half = rows // 2
    block = half // len(order)
    more = rest is None
    last = w_down.shape[1] - weight.shape[1]
    return pl.pallas_call(
        functools.partial(down_body, order, block, start, more),
        out_shape=[pltpu.VMEM((half, step), BF16)] * 2
        + ([pltpu.VMEM((depth, last), BF16)] if more else []),
        in_specs=[VMEM_FULL] * 2 + [ANY_FULL if more else VMEM_FULL],
        out_specs=[VMEM_FULL] * (3 if more else 2),
        scratch_shapes=[pltpu.SemaphoreType.DMA((8,))] if more else [],
        compiler_params=scoped,
        cost_estimate=cost(2 * rows * depth * step, 2 * depth * step),
    )(in_vmem(hidden), in_vmem(weight), in_hbm(w_down) if more else in_vmem(rest))


def pair_body(keep_ref, got_ref, *outs):
    rows = outs[0].shape[0]
    for k, out in enumerate(outs):
        at = slice(k * rows, (k + 1) * rows)
        out[...] = (keep_ref[at].astype(F32) + got_ref[at].astype(F32)).astype(BF16)


def pair_call(keep, got, rows, scoped):
    count = keep.shape[0] // rows
    return pl.pallas_call(
        pair_body,
        out_shape=[pltpu.VMEM((rows, keep.shape[1]), BF16)] * count,
        in_specs=[VMEM_FULL] * 2,
        out_specs=[VMEM_FULL] * count,
        compiler_params=scoped,
    )(in_vmem(keep), in_vmem(got))


def add_body(left_ref, right_ref, out_ref):
    total = left_ref[...].astype(F32) + right_ref[...].astype(F32)
    out_ref[...] = total.astype(out_ref.dtype)


def add_call(left, right, scoped, kind=BF16):
    return pl.pallas_call(
        add_body,
        out_shape=pltpu.VMEM(left.shape, kind),
        in_specs=[VMEM_FULL] * 2,
        out_specs=VMEM_FULL,
        compiler_params=scoped,
    )(in_vmem(left), in_vmem(right))


def finish_body(counts, *refs):
    ins, out_ref = refs[:-1], refs[-1]
    start = 0
    for count in counts:
        terms, ins = ins[:count], ins[count:]
        stop = start + terms[0].shape[1]
        total = terms[0][...].astype(F32)
        for ref in terms[1:]:
            total = total + ref[...].astype(F32)
        out_ref[:, start:stop] = total.astype(BF16)
        start = stop


def finish_call(chunks, rows, width, scoped):
    parts = [p for chunk in chunks for p in chunk]
    return pl.pallas_call(
        functools.partial(finish_body, [len(chunk) for chunk in chunks]),
        out_shape=jax.ShapeDtypeStruct((rows, width), BF16),
        in_specs=[VMEM_FULL] * len(parts),
        out_specs=VMEM_FULL,
        compiler_params=scoped,
    )(*[in_vmem(p) for p in parts])


def per_device(tokens, norm_gain, expert_ids, gate_prob, w_gate, w_up, w_down):
    rows, width = tokens.shape
    local, _, hidden = w_gate.shape
    size = lax.axis_size("exp") * lax.axis_size("ten")
    expert_count = local * lax.axis_size("exp")
    far = range(2, size, 2)
    w_rows = w_down.reshape(local * hidden, width)

    scoped = params(size * rows, width)

    own = norm_call(tokens, norm_gain, expert_ids, gate_prob, expert_count, scoped)
    ours = [own, exchange(own, size, 1)]
    *slots, early, fetched = fetch_call(ours, w_gate, w_up, expert_count, scoped)
    near = [after(exchange(own, size, mask), fetched) for mask in far]
    pieces = ours + near + [exchange(piece, size, 1) for piece in near]
    order = [(0, 1)] + [(2 + i, 2 + len(far) + i) for i in range(len(far))]
    mixed_hidden, weight = gate_up_call(
        pieces, early, *slots, w_gate, w_up, w_rows, expert_count, scoped
    )
    step = width // 2
    keep_a, send_a, rest = down_call(0, step, mixed_hidden, weight, w_rows, None, order, scoped)
    keep_b, send_b = down_call(step, width - step, mixed_hidden, weight, w_rows, rest, order, scoped)
    got_a, got_b = exchange(send_a, size, 1), exchange(send_b, size, 1)
    blocks_a = pair_call(keep_a, got_a, rows, scoped)
    blocks_b = pair_call(keep_b, got_b, rows, scoped)
    if len(blocks_a) != 4:
        chunks = []
        for blocks in (blocks_a, blocks_b):
            sent = [exchange(b, size, mask) for b, mask in zip(blocks[1:], far)]
            chunks.append([blocks[0], *sent])
        return finish_call(chunks, rows, width, scoped)

    def over(block, axis):
        return exchange(block, size, far[axis])

    own_a, first_a, second_a, both_a = blocks_a
    own_b, first_b, second_b, both_b = blocks_b
    passed_a = over(both_a, 1)
    direct_a = over(second_a, 1)
    passed_b = over(both_b, 0)
    direct_b = over(first_b, 0)
    summed_a = over(add_call(first_a, passed_a, scoped), 0)
    summed_b = over(add_call(second_b, passed_b, scoped), 1)
    chunks = [
        [add_call(own_a, direct_a, scoped, F32), summed_a],
        [add_call(own_b, direct_b, scoped, F32), summed_b],
    ]
    return finish_call(chunks, rows, width, scoped)


def solution(mesh):
    placed = (
        P(("grp", "exp", "ten"), None),
        P(),
        P(("grp", "exp", "ten"), None),
        P(("grp", "exp", "ten"), None),
        P("exp", None, "ten"),
        P("exp", None, "ten"),
        P("exp", "ten", None),
    )
    return jax.shard_map(
        per_device,
        mesh=mesh,
        in_specs=placed,
        out_specs=P(("grp", "exp", "ten"), None),
        check_vma=False,
    )
```
